32 devices in a mesh: grp: 2 (over x), tp: 4 (over y, core), dp: 4 (over z).
Axes of the slice: x: 2, y: 2, z: 4, core: 2. Of those that a mesh axis runs over, the one named last changes fastest.
Arguments:
- prompt: bfloat16 [8192, 8192], P(('grp', 'dp'), 'tp'), parts along dimension 0, may hold values from -6 to 6
- query_weight: bfloat16 [8192, 4096], P(None, 'tp'), may hold values from -0.0625 to 0.0625
- key_value_weight: bfloat16 [8192, 512], P(None, 'tp'), may hold values from -0.0625 to 0.0625
- adapter_down_weight: bfloat16 [8192, 64, 16], P('tp'), may hold values from -0.0625 to 0.0625
- query_up_weight: bfloat16 [64, 16, 4096], P(None, None, 'tp'), may hold values from -1.5 to 1.5
- adapter_up_weight: bfloat16 [64, 16, 512], P(None, None, 'tp'), may hold values from -1.5 to 1.5
- tenant: int32 [8192], P(('grp', 'dp')), parts along dimension 0, may hold values from 0 to 63
- page_destination_slot: int32 [512], P(('grp', 'dp')), parts along dimension 0, may hold values from 0 to 255, as said below
- key_value_cache: bfloat16 [8, 4, 256, 16, 256], P(('grp', 'dp'), 'tp'), parts along dimension 0, as said below
- queries: bfloat16 [8, 4, 16, 1024], P(('grp', 'dp'), 'tp'), parts along dimension 0, as said below
- request_page_table: int32 [256, 16], P(('grp', 'dp')), parts along dimension 0, may hold values from 0 to 287, as said below
- context_length: int32 [256], P(('grp', 'dp')), parts along dimension 0, may hold values from 33 to 256, as said below
Outputs:
- attention: bfloat16 [8, 4, 16, 1024], P(('grp', 'dp'), 'tp'), parts along dimension 0
- prompt_queries: bfloat16 [8192, 4096], P(('grp', 'dp'), 'tp'), parts along dimension 0
The draws below stay inside these ranges and needn't reach their ends.
There are 2 independent parts, one for each index of `grp`. The reference program is written for one: setup_inputs(seed, part) draws one part's arguments, and reference() takes and returns one part's arrays. A program takes and returns all parts, laid end to end along the dimension named above; an argument that names none is the same for every part. Nothing has to cross between parts.
Inputs may be any that keep to these rules, and one draw needn't show every extreme that they name: `page_destination_slot`: A permutation. Entry p of replica i's 64 entries is o * 64 + s * 32 + q: page p of replica i goes to slot q of half s of replica o; every replica sends exactly 8 pages to each half of each replica. key_value_cache: entries of order one. queries: entries of order one for most requests; a few requests may hold much larger queries. `request_page_table`: entries below 256 are resident pages, 256 + q new slot q. A request using n pages has its last 2 used entries new, each new slot of a replica's half used by exactly one request; entries past the used pages are arbitrary pages. A request's pages in use are ceil(context_length / 16).
All inputs are finite; a program needn't handle non-finite values.
Results may differ from the reference program's by a relative error of at most 0.0062.
Values may be sent and summed in bfloat16 or wider, within the bound.
A program may use at most 128 MiB of HBM per device.

```python
import math
import jax
import jax.numpy as jnp
import numpy as np
from jax import lax

MODEL_WIDTH = 8192
HEAD = 128
GROUP = 8
ADAPTER_RANK = 16
TENANT_COUNT = 64
PAGE = 16
MAXP = 16
TOK_DEV = 1024
ROWS_DEV = 32
KVH = 2
KEY_VALUE_COLUMNS = 512
QCOLS = 4096
TOKENS = 4096
PP = 64
NEWP = 32
PPE = 8
HALF = 16
NEWR = 2
POOL = 256
CTX = 256
N_TP = 4
N_DP = 4


def page_layout(key):
    key = jax.random.fold_in(key, 11)
    first_key, second_key, third_key, fourth_key = jax.random.split(key, 4)
    row_total = N_DP * ROWS_DEV
    used = jax.random.randint(first_key, (row_total,), NEWR + 1, MAXP + 1)
    local_row = jnp.arange(row_total) % ROWS_DEV
    used = jnp.where(local_row == 0, MAXP, used)
    last_fill = jax.random.randint(second_key, (row_total,), 1, PAGE + 1)
    last_fill = jnp.where(local_row == 0, PAGE, last_fill)
    lengths = (used - 1) * PAGE + last_fill
    resident = jax.random.randint(third_key, (row_total, MAXP), 0, POOL)
    slot_keys = jax.random.split(fourth_key, N_DP * 2)
    slot_perm = jax.vmap(lambda subkey: jax.random.permutation(subkey, NEWP))(slot_keys)
    slot_perm = slot_perm.reshape(row_total, NEWR)
    column = jnp.arange(MAXP)[None, :]
    first_new = (used - NEWR)[:, None]
    offset = jnp.clip(column - first_new, 0, NEWR - 1)
    new_ids = POOL + jnp.take_along_axis(slot_perm, offset, axis=1)
    row_table = jnp.where((column >= first_new) & (column < used[:, None]), new_ids, resident)
    return (row_table.astype(jnp.int32), lengths.astype(jnp.int32))


def cache_base(key):
    key = jax.random.fold_in(key, 23)
    return jax.random.normal(key, (N_DP, N_TP, POOL, PAGE, 2 * HEAD), jnp.float32)


def draw_request_page_table(key, part):
    row_table, lengths = page_layout(key)
    return row_table


def draw_context_length(key, part):
    row_table, lengths = page_layout(key)
    return lengths


def draw_key_value_cache(key, part):
    resident = cache_base(key)
    return resident.astype(jnp.bfloat16)


def draw_queries(key, part):
    key = jax.random.fold_in(key, 7)
    array_shape = (N_DP, N_TP, HALF, GROUP * HEAD)
    return jax.random.normal(key, array_shape, jnp.float32).astype(jnp.bfloat16)


def draw_page_destination_slot(key, part):
    key = jax.random.fold_in(key, 31)
    first_key, second_key = jax.random.split(key)
    slot_perm = jax.vmap(lambda subkey: jax.random.permutation(subkey, NEWP))(jax.random.split(first_key, N_DP * 2))
    slot_perm = slot_perm.reshape(N_DP, 2, N_DP, PPE)
    owner = jnp.arange(N_DP)[:, None, None, None]
    side = jnp.arange(2)[None, :, None, None]
    target = owner * PP + side * NEWP + slot_perm
    target = jnp.transpose(target, (2, 0, 1, 3)).reshape(N_DP, PP)
    shuffle = jax.vmap(lambda subkey: jax.random.permutation(subkey, PP))(jax.random.split(second_key, N_DP))
    target = jnp.take_along_axis(target, shuffle, axis=1)
    return target.reshape(N_DP * PP).astype(jnp.int32)


def plant(values, own_key, least, top_value):
    longest = values.shape.index(max(values.shape))
    spots = []
    for shift in (0, 1):
        where = [jax.random.randint(jax.random.fold_in(own_key, axis), (), 0, length) for axis, length in enumerate(values.shape)]
        where[longest] = (where[longest] + shift) % values.shape[longest]
        spots.append(tuple(where))
    return values.at[spots[0]].set(least).at[spots[1]].set(top_value)


def steps_of(rng, dims, cuts, smallest, top_value):
    level, own = 1.0, jax.random.fold_in(rng, 6)
    for dim, blocks in cuts:
        heights = jnp.exp(jax.random.uniform(jax.random.fold_in(own, dim), (blocks,), jnp.float32, smallest / len(cuts), top_value / len(cuts)))
        level = level * jnp.repeat(heights, dims[dim] // blocks).reshape([-1 if axis == dim else 1 for axis in range(len(dims))])
    return level


def cumulative_ranks(count, slope):
    loads = [(1 << 20) // math.isqrt(standing ** slope) + 1 for standing in range(1, count + 1)]
    scale = 1 + sum(loads) // (1 << 30)
    return np.cumsum(np.array([max(1, weight // scale) for weight in loads]))


def ranked_ids(rng, shape, number_of, skew):
    listing = cumulative_ranks(number_of, skew)
    lot = jax.random.randint(jax.random.fold_in(rng, 1), shape, 0, int(listing[number_of - 1]))
    rank = jnp.searchsorted(jnp.asarray(listing, jnp.int32), lot, side="right")
    return jax.random.permutation(jax.random.fold_in(rng, 2), number_of)[rank].astype(jnp.int32)


def normal_values(own_key, extent, deviation, reach, pieces=(), dtype=jnp.bfloat16):
    loudness = steps_of(own_key, extent, pieces, -0.22, 0.18) if pieces else 1.0
    values = jax.random.normal(own_key, extent, jnp.float32) * deviation * loudness
    return jnp.minimum(jnp.maximum(values, -reach), reach).astype(dtype)


def setup_inputs(seed: int = 0, part: int = 0) -> dict:
    seeds = jax.random.split(jax.random.key(seed), 13)
    part_keys = jax.random.split(jax.random.fold_in(seeds[12], part), 13)
    return {
        "prompt": normal_values(part_keys[0], (TOKENS, MODEL_WIDTH), 1.0, 6.0, ((0, 4), (1, 4))),
        "query_weight": normal_values(seeds[1], (MODEL_WIDTH, QCOLS), MODEL_WIDTH ** -0.5, 0.0625, ((1, 4),)),
        "key_value_weight": normal_values(seeds[2], (MODEL_WIDTH, KEY_VALUE_COLUMNS), MODEL_WIDTH ** -0.5, 0.0625, ((1, 4),)),
        "adapter_down_weight": normal_values(seeds[3], (MODEL_WIDTH, TENANT_COUNT, ADAPTER_RANK), MODEL_WIDTH ** -0.5, 0.0625, ((0, 4),)),
        "query_up_weight": normal_values(seeds[4], (TENANT_COUNT, ADAPTER_RANK, QCOLS), ADAPTER_RANK ** -0.5, 1.5, ((2, 4),)),
        "adapter_up_weight": normal_values(seeds[5], (TENANT_COUNT, ADAPTER_RANK, KEY_VALUE_COLUMNS), ADAPTER_RANK ** -0.5, 1.5, ((2, 4),)),
        "tenant": plant(ranked_ids(part_keys[6], (TOKENS,), TENANT_COUNT, 2), jax.random.fold_in(part_keys[6], 3), 0, TENANT_COUNT - 1).astype(jnp.int32),
        "page_destination_slot": draw_page_destination_slot(jax.random.fold_in(jax.random.fold_in(seeds[12], part), 71), part),
        "key_value_cache": draw_key_value_cache(jax.random.fold_in(jax.random.fold_in(seeds[12], part), 71), part),
        "queries": draw_queries(jax.random.fold_in(jax.random.fold_in(seeds[12], part), 71), part),
        "request_page_table": draw_request_page_table(jax.random.fold_in(jax.random.fold_in(seeds[12], part), 71), part),
        "context_length": draw_context_length(jax.random.fold_in(jax.random.fold_in(seeds[12], part), 71), part),
    }


def reference(prompt, query_weight, key_value_weight, adapter_down_weight, query_up_weight, adapter_up_weight, tenant, page_destination_slot, key_value_cache, queries, request_page_table, context_length):
    block_count = TOKENS // 128

    def shrink_block(item):
        token_rows, tenant_index = item
        down_matrices = jnp.take(adapter_down_weight, tenant_index, axis=1).astype(jnp.float32)
        return jnp.einsum('td,dtr->tr', token_rows.astype(jnp.float32), down_matrices)
    shrink = lax.map(shrink_block, (prompt.reshape(block_count, 128, MODEL_WIDTH), tenant.reshape(block_count, 128)))
    shrink = lax.optimization_barrier(shrink.reshape(TOKENS, ADAPTER_RANK).astype(jnp.bfloat16))
    all_up_weight = jnp.concatenate([query_up_weight, adapter_up_weight], -1)

    def expand_block(item):
        low_rows, tenant_index = item
        up_maps = jnp.take(all_up_weight, tenant_index, axis=0).astype(jnp.float32)
        return jnp.einsum('tr,trc->tc', low_rows.astype(jnp.float32), up_maps)
    adapted = lax.map(expand_block, (shrink.reshape(block_count, 128, ADAPTER_RANK), tenant.reshape(block_count, 128)))
    adapted = adapted.reshape(TOKENS, QCOLS + KEY_VALUE_COLUMNS)
    query_base = lax.map(lambda token_rows: jnp.dot(token_rows, query_weight, preferred_element_type=jnp.float32), prompt.reshape(N_DP, TOK_DEV, MODEL_WIDTH)).reshape(TOKENS, QCOLS)
    prompt_queries = (query_base + 0.5 * adapted[:, :QCOLS]).astype(jnp.bfloat16)
    base_proj = lax.map(lambda token_rows: jnp.dot(token_rows, key_value_weight, preferred_element_type=jnp.float32), prompt.reshape(N_DP, TOK_DEV, MODEL_WIDTH)).reshape(TOKENS, KEY_VALUE_COLUMNS)
    fresh = (base_proj + 0.5 * adapted[:, QCOLS:]).astype(jnp.bfloat16).reshape(N_DP * PP, PAGE, KEY_VALUE_COLUMNS)
    placed = jnp.zeros_like(fresh).at[page_destination_slot].set(fresh)
    placed = lax.optimization_barrier(placed.reshape(N_DP, 2, NEWP, PAGE, KVH, 2 * HEAD))
    row_tables = request_page_table.reshape(N_DP, 2, HALF, MAXP)
    row_lengths = context_length.reshape(N_DP, 2, HALF)

    def attend(flat_index):
        replica = flat_index // N_TP
        device = flat_index % N_TP
        kv_head = device // 2
        side = device % 2
        new_part = placed[replica, side][:, :, kv_head, :]
        page_pool = jnp.concatenate([key_value_cache[replica, device], new_part], 0)
        gathered = page_pool[row_tables[replica, side]].reshape(HALF, CTX, 2 * HEAD).astype(jnp.float32)
        query_part = queries[replica, device].reshape(HALF, GROUP, HEAD).astype(jnp.float32)
        scores = jnp.einsum('rgd,rcd->rgc', query_part, gathered[..., :HEAD]) / math.sqrt(HEAD)
        inside = jnp.arange(CTX)[None, None, :] < row_lengths[replica, side][:, None, None]
        scores = jnp.where(inside, scores, -jnp.inf)
        weights = lax.optimization_barrier(jax.nn.softmax(scores, axis=-1).astype(jnp.bfloat16))
        attended = jnp.einsum('rgc,rcd->rgd', weights.astype(jnp.float32), gathered[..., HEAD:])
        return attended.reshape(HALF, GROUP * HEAD).astype(jnp.bfloat16)
    outputs = lax.map(attend, jnp.arange(N_DP * N_TP))
    return (outputs.reshape(N_DP, N_TP, HALF, GROUP * HEAD), prompt_queries)
```

```python
import functools
import math

import jax
import jax.numpy as jnp
from jax import lax
from jax.experimental import pallas as pl
from jax.experimental.pallas import tpu as pltpu
from jax.sharding import PartitionSpec as P

PAGE = 16
CHUNK = 128
BLOCK = 1024
NEG = -1e30
F32 = jnp.float32
BF16 = jnp.bfloat16


def nt_dot(a, b):
    return lax.dot_general(a, b, (((1,), (1,)), ((), ())), preferred_element_type=F32)


def dot(a, b):
    return jnp.dot(a, b, preferred_element_type=F32)


def kernel(
    n_tp,
    n_dp,
    pool,
    x_hbm,
    wq_hbm,
    wkv_hbm,
    wd_hbm,
    wup_hbm,
    wkup_hbm,
    tenant,
    slots,
    meta,
    cache_hbm,
    queries,
    out_a,
    out_q,
    xg,
    wq,
    wkv,
    wd,
    wup,
    wkup,
    cache,
    oq,
    kv,
    shp,
    shrink,
    slots_all,
    counts,
    qs,
    o_acc,
    m_acc,
    l_acc,
    acc_q,
    load_sem,
    xload_sem,
    sib_send,
    sib_recv,
    far_send,
    far_recv,
    fwd_send,
    fwd_recv,
    shr_send,
    shr_recv,
    slot_send,
    slot_recv,
    page_send,
    page_recv,
    out_sem,
):
    me = lax.axis_index("tp")
    dp = lax.axis_index("dp")
    kind = lax.rem(me, 2)
    sib = me + 1 - 2 * kind
    tok = x_hbm.shape[0]
    n_chunk = tok // CHUNK
    n_y = n_tp // 2
    tenants = wd.shape[0] // 16

    def rows(k):
        return pl.ds(pl.multiple_of(k * CHUNK, CHUNK), CHUNK)

    def remote(src, dst, ss, rs, tp_id, dp_id):
        return pltpu.make_async_remote_copy(
            src_ref=src,
            dst_ref=dst,
            send_sem=ss,
            recv_sem=rs,
            device_id={"tp": tp_id, "dp": dp_id},
            device_id_type=pl.DeviceIdType.MESH,
        )

    barrier = pltpu.get_barrier_semaphore()
    n_peers = n_tp - 1 + 2 * (n_dp - 1)
    for d in range(1, n_tp):
        pl.semaphore_signal(
            barrier,
            inc=1,
            device_id={"tp": lax.rem(me + d, n_tp), "dp": dp},
            device_id_type=pl.DeviceIdType.MESH,
        )
    for d in range(1, n_dp):
        for t in (me, sib):
            pl.semaphore_signal(
                barrier,
                inc=1,
                device_id={"tp": t, "dp": lax.rem(dp + d, n_dp)},
                device_id_type=pl.DeviceIdType.MESH,
            )

    own_load = pltpu.make_async_copy(x_hbm, xg.at[me], xload_sem)
    own_load.start()
    loads = [
        pltpu.make_async_copy(src, dst, load_sem.at[i])
        for i, (src, dst) in enumerate(
            (
                (wd_hbm, wd),
                (cache_hbm, cache),
                (wkv_hbm, wkv),
                (wup_hbm, wup),
                (wkup_hbm, wkup),
                (wq_hbm, wq),
            )
        )
    ]
    for load in loads:
        load.start()

    pl.semaphore_wait(barrier, n_peers)

    def to_sibling(k):
        return remote(
            x_hbm.at[rows(k)], xg.at[me, rows(k)], sib_send.at[k], sib_recv.at[k], sib, dp
        )

    def from_sibling(k):
        return remote(
            x_hbm.at[rows(k)], xg.at[sib, rows(k)], sib_send.at[k], sib_recv.at[k], sib, dp
        )

    def far_to(y):
        return lax.rem(me + 2 * y, n_tp)

    def far_from(y):
        return lax.rem(me + n_tp - 2 * y, n_tp)

    def to_far(k, y):
        return remote(
            x_hbm.at[rows(k)],
            xg.at[me, rows(k)],
            far_send.at[k, y - 1],
            far_recv.at[k, y - 1],
            far_to(y),
            dp,
        )

    def from_far(k, y):
        return remote(
            x_hbm.at[rows(k)],
            xg.at[far_from(y), rows(k)],
            far_send.at[k, y - 1],
            far_recv.at[k, y - 1],
            far_to(y),
            dp,
        )

    def pass_on(k, y):
        block = xg.at[far_from(y), rows(k)]
        return remote(block, block, fwd_send.at[k, y - 1], fwd_recv.at[k, y - 1], sib, dp)

    def passed(k, y):
        src = lax.rem(sib + n_tp - 2 * y, n_tp)
        block = xg.at[src, rows(k)]
        return remote(block, block, fwd_send.at[k, y - 1], fwd_recv.at[k, y - 1], sib, dp)

    def to_shrink(d):
        return remote(
            shp.at[me],
            shp.at[me],
            shr_send.at[d - 1],
            shr_recv.at[d - 1],
            lax.rem(me + d, n_tp),
            dp,
        )

    def from_shrink(d):
        src = lax.rem(me + n_tp - d, n_tp)
        return remote(shp.at[src], shp.at[src], shr_send.at[d - 1], shr_recv.at[d - 1], src, dp)

    def to_slots(d):
        return remote(
            slots,
            slots_all.at[dp],
            slot_send.at[d - 1],
            slot_recv.at[d - 1],
            me,
            lax.rem(dp + d, n_dp),
        )

    def from_slots(d):
        src = lax.rem(dp + n_dp - d, n_dp)
        return remote(
            slots, slots_all.at[src], slot_send.at[d - 1], slot_recv.at[d - 1], me, src
        )

    def page_copy(k, which, other, d, replica, target_tp, target_dp):
        block = kv.at[which, replica, rows(k)]
        index = other * n_dp + d
        return remote(
            block, block, page_send.at[k, index], page_recv.at[k, index], target_tp, target_dp
        )

    def page_pairs():
        return [(other, d) for other in (0, 1) for d in range(n_dp) if other or d]

    def to_pages(k, other, d):
        target = sib if other else me
        return page_copy(k, kind, other, d, dp, target, lax.rem(dp + d, n_dp))

    def from_pages(k, other, d):
        which = 1 - kind if other else kind
        src = lax.rem(dp + n_dp - d, n_dp)
        return page_copy(k, which, other, d, src, sib, src)

    for k in range(2):
        for y in range(1, n_y):
            to_far(k, y).start()

    @pl.loop(0, n_chunk)
    def _(k):
        to_sibling(k).start()

    for d in range(1, n_dp):
        to_slots(d).start()
    slots_all[dp] = slots[...]

    own_load.wait()
    loads[0].wait()
    wide = 2 * CHUNK

    @pl.loop(0, tok // wide)
    def _(b):
        cols = pl.ds(pl.multiple_of(b * wide, wide), wide)
        spread = nt_dot(wd[...], xg[me, cols, :])
        group = lax.broadcasted_iota(jnp.int32, spread.shape, 0) // 16
        kept = jnp.where(group == tenant[:, cols], spread, 0.0)
        shp[me, :, cols] = jnp.sum(kept.reshape(tenants, 16, wide), axis=0)

    for d in range(1, n_tp):
        to_shrink(d).start()

    lengths = meta[pl.ds(pl.multiple_of(kind * 16, 16), 16), 16:17]
    table = meta[pl.ds(pl.multiple_of(kind * 16, 16), 16), 0:16]
    inv_scale = 1.0 / math.sqrt(128)

    def count_of(page_ids):
        lane = lax.broadcasted_iota(jnp.int32, (16, BLOCK), 1)
        offset = lane % PAGE
        total = jnp.zeros((16, BLOCK), F32)
        for p in range(16):
            hit = (table[:, p : p + 1] == page_ids) & (offset + p * PAGE < lengths)
            total += jnp.where(hit, 1.0, 0.0)
        return total

    def scores_of(keys, count):
        s = nt_dot(qs[...], keys).reshape(8, 16, BLOCK) * inv_scale
        return jnp.where(count[None] > 0, s, NEG)

    def weigh(s, count, m, values):
        p = count[None] * jnp.exp(s - m)
        l = jnp.sum(p, axis=2, keepdims=True)
        o = dot(p.reshape(128, BLOCK).astype(BF16), values)
        return l, o.reshape(8, 16, 128)

    for g in range(8):
        qs[g * 16 : (g + 1) * 16, :] = queries[:, g * 128 : (g + 1) * 128]
    m_acc[...] = jnp.full(m_acc.shape, NEG, F32)
    l_acc[...] = jnp.zeros(l_acc.shape, F32)
    o_acc[...] = jnp.zeros(o_acc.shape, F32)
    loads[1].wait()

    @pl.loop(0, pool * PAGE // BLOCK)
    def _(b):
        cols = pl.ds(pl.multiple_of(b * BLOCK, BLOCK), BLOCK)
        lane = lax.broadcasted_iota(jnp.int32, (16, BLOCK), 1)
        count = count_of((lane + b * BLOCK) // PAGE)
        s = scores_of(cache[cols, :128], count)
        m_old = m_acc[...]
        m = jnp.maximum(m_old, jnp.max(s, axis=2, keepdims=True))
        l, o = weigh(s, count, m, cache[cols, 128:])
        alpha = jnp.exp(m_old - m)
        m_acc[...] = m
        l_acc[...] = l_acc[...] * alpha + l
        o_acc[...] = o_acc[...] * alpha + o

    for d in range(1, n_dp):
        from_slots(d).wait_recv()
    new_pages = tok // PAGE // 2

    @pl.loop(0, n_dp)
    def _(i):
        dest = slots_all[i, 0:1, :]
        mine = dest // new_pages == dp * 2 + kind
        page_ids = jnp.where(mine, dest % new_pages + pool, -1)
        counts[i] = count_of(page_ids)

    for d in range(1, n_tp):
        from_shrink(d).wait_recv()
    total = shp[0]
    for t in range(1, n_tp):
        total = total + shp[t]
    shrink[...] = total.astype(BF16).astype(F32)
    for load in loads[2:]:
        load.wait()

    @pl.loop(0, n_chunk)
    def _(k):
        cols = rows(k)
        from_sibling(k).wait_recv()
        low = jnp.broadcast_to(shrink[:, cols][None], (tenants, 16, CHUNK))
        low = low.reshape(tenants * 16, CHUNK)
        group = lax.broadcasted_iota(jnp.int32, low.shape, 0) // 16
        widened = jnp.where(group == tenant[:, cols], low, 0.0).T.astype(BF16)
        acc_kv = 0.5 * dot(widened, wkup[...])
        acc_q[...] = 0.5 * dot(widened, wup[...])
        for src in (me, sib):
            acc_kv += dot(xg[src, cols, :], wkv[src])
            acc_q[...] += dot(xg[src, cols, :], wq[src])
        for y in range(1, n_y):
            from_far(k, y).wait_recv()
            pass_on(k, y).start()

        @pl.when(k + 2 < n_chunk)
        def _():
            for y in range(1, n_y):
                to_far(k + 2, y).start()

        for y in range(1, n_y):
            src = far_from(y)
            acc_kv += dot(xg[src, cols, :], wkv[src])
        for y in range(1, n_y):
            passed(k, y).wait_recv()
            src = lax.rem(sib + n_tp - 2 * y, n_tp)
            acc_kv += dot(xg[src, cols, :], wkv[src])
        kv[kind, dp, cols, :] = acc_kv.astype(BF16)
        for other, d in page_pairs():
            to_pages(k, other, d).start()
        for y in range(1, n_y):
            for base in (me, sib):
                src = lax.rem(base + n_tp - 2 * y, n_tp)
                acc_q[...] += dot(xg[src, cols, :], wq[src])
        oq[cols, :] = acc_q[...].astype(BF16)
        pltpu.make_async_copy(oq.at[cols], out_q.at[cols], out_sem.at[k]).start()

    @pl.loop(0, n_chunk)
    def _(k):
        for other, d in page_pairs():
            from_pages(k, other, d).wait_recv()

    parts = [scores_of(kv[0, i], counts[i]) for i in range(n_dp)]
    m_old = m_acc[...]
    m = m_old
    for s in parts:
        m = jnp.maximum(m, jnp.max(s, axis=2, keepdims=True))
    alpha = jnp.exp(m_old - m)
    l_sum = l_acc[...] * alpha
    o_sum = o_acc[...] * alpha
    for i, s in enumerate(parts):
        l, o = weigh(s, counts[i], m, kv[1, i])
        l_sum += l
        o_sum += o
    result = (o_sum / l_sum).astype(BF16)
    for g in range(8):
        out_a[:, g * 128 : (g + 1) * 128] = result[g]

    for d in range(1, n_dp):
        to_slots(d).wait_send()
    for d in range(1, n_tp):
        to_shrink(d).wait_send()

    @pl.loop(0, n_chunk)
    def _(k):
        to_sibling(k).wait_send()
        for y in range(1, n_y):
            to_far(k, y).wait_send()
            pass_on(k, y).wait_send()
        for other, d in page_pairs():
            to_pages(k, other, d).wait_send()
        pltpu.make_async_copy(oq.at[rows(k)], out_q.at[rows(k)], out_sem.at[k]).wait()


def per_device(
    n_tp,
    n_dp,
    prompt,
    query_weight,
    key_value_weight,
    adapter_down_weight,
    query_up_weight,
    adapter_up_weight,
    tenant,
    page_destination_slot,
    key_value_cache,
    queries,
    request_page_table,
    context_length,
):
    tok, feat = prompt.shape
    head = key_value_weight.shape[1]
    qcols = query_weight.shape[1]
    tenants, rank = adapter_down_weight.shape[1:]
    ranks = tenants * rank
    pool = key_value_cache.shape[2]
    half = queries.shape[2]
    n_chunk = tok // CHUNK
    down = adapter_down_weight.transpose(1, 2, 0).reshape(ranks, feat)
    slots = jnp.broadcast_to(jnp.repeat(page_destination_slot, PAGE)[None, :], (8, tok))
    meta = jnp.concatenate([request_page_table, context_length[:, None]], axis=1)
    hbm = pl.BlockSpec(memory_space=pl.ANY)
    vmem = pl.BlockSpec(memory_space=pltpu.VMEM)
    dma = pltpu.SemaphoreType.DMA
    n_far = n_tp // 2 - 1
    out_a, out_q = pl.pallas_call(
        functools.partial(kernel, n_tp, n_dp, pool),
        out_shape=(
            jax.ShapeDtypeStruct((half, queries.shape[3]), BF16),
            jax.ShapeDtypeStruct((tok, qcols), BF16),
        ),
        in_specs=[hbm] * 6 + [vmem] * 3 + [hbm, vmem],
        out_specs=(vmem, hbm),
        scratch_shapes=[
            pltpu.VMEM((n_tp, tok, feat), BF16),
            pltpu.VMEM((n_tp, feat, qcols), BF16),
            pltpu.VMEM((n_tp, feat, head), BF16),
            pltpu.VMEM((ranks, feat), BF16),
            pltpu.VMEM((ranks, qcols), BF16),
            pltpu.VMEM((ranks, head), BF16),
            pltpu.VMEM((pool * PAGE, 2 * head), BF16),
            pltpu.VMEM((tok, qcols), BF16),
            pltpu.VMEM((2, n_dp, tok, head), BF16),
            pltpu.VMEM((n_tp, rank, tok), F32),
            pltpu.VMEM((rank, tok), F32),
            pltpu.VMEM((n_dp, 8, tok), jnp.int32),
            pltpu.VMEM((n_dp, half, tok), F32),
            pltpu.VMEM((8 * half, head), BF16),
            pltpu.VMEM((8, half, head), F32),
            pltpu.VMEM((8, half, 1), F32),
            pltpu.VMEM((8, half, 1), F32),
            pltpu.VMEM((CHUNK, qcols), F32),
            dma((6,)),
            dma,
            dma((n_chunk,)),
            dma((n_chunk,)),
            dma((n_chunk, n_far)),
            dma((n_chunk, n_far)),
            dma((n_chunk, n_far)),
            dma((n_chunk, n_far)),
            dma((n_tp - 1,)),
            dma((n_tp - 1,)),
            dma((n_dp - 1,)),
            dma((n_dp - 1,)),
            dma((n_chunk, 2 * n_dp)),
            dma((n_chunk, 2 * n_dp)),
            dma((n_chunk,)),
        ],
        compiler_params=pltpu.CompilerParams(
            collective_id=0, has_side_effects=True, vmem_limit_bytes=63 * 2**20
        ),
        name="serve_layer",
    )(
        prompt,
        query_weight.reshape(n_tp, feat, qcols),
        key_value_weight.reshape(n_tp, feat, head),
        down,
        query_up_weight.reshape(ranks, qcols),
        adapter_up_weight.reshape(ranks, head),
        tenant[None, :],
        slots,
        meta,
        key_value_cache.reshape(pool * PAGE, 2 * head),
        queries.reshape(half, -1),
    )
    return out_a.reshape(1, 1, half, -1), out_q


def solution(mesh):
    in_specs = (
        P(("grp", "dp"), "tp"),
        P(None, "tp"),
        P(None, "tp"),
        P("tp", None, None),
        P(None, None, "tp"),
        P(None, None, "tp"),
        P(("grp", "dp")),
        P(("grp", "dp")),
        P(("grp", "dp"), "tp", None, None, None),
        P(("grp", "dp"), "tp", None, None),
        P(("grp", "dp"), None),
        P(("grp", "dp")),
    )
    out_specs = (P(("grp", "dp"), "tp", None, None), P(("grp", "dp"), "tp"))
    return jax.shard_map(
        functools.partial(per_device, mesh.shape["tp"], mesh.shape["dp"]),
        mesh=mesh,
        in_specs=in_specs,
        out_specs=out_specs,
        check_vma=False,
    )
```

```python
import functools
import math

import jax
import jax.numpy as jnp
from jax import lax
from jax.experimental import pallas as pl
from jax.experimental.pallas import tpu as pltpu
from jax.sharding import PartitionSpec as P

PAGE = 16
CHUNK = 128
SUB = 32
AHEAD = 3
BLOCK = 1024
NEG = -1e30
F32 = jnp.float32
BF16 = jnp.bfloat16


def nt_dot(a, b):
    return lax.dot_general(a, b, (((1,), (1,)), ((), ())), preferred_element_type=F32)


def exact_nt(a, b):
    return lax.dot_general(
        a,
        b,
        (((1,), (1,)), ((), ())),
        preferred_element_type=F32,
        precision=lax.Precision.HIGHEST,
    )


def dot(a, b):
    return jnp.dot(a, b, preferred_element_type=F32)


def kernel(
    n_tp,
    n_dp,
    pool,
    x_hbm,
    wq_hbm,
    wkv_hbm,
    wd_hbm,
    wup_hbm,
    wkup_hbm,
    tenant,
    slots,
    table_t,
    context,
    cache_hbm,
    queries,
    out_a,
    out_q,
    xg,
    wq,
    wkv,
    wd,
    wup,
    wkup,
    cache,
    oq,
    kv,
    pair,
    shp,
    shrink,
    slots_all,
    slots_own,
    counts,
    qs,
    o_acc,
    m_acc,
    l_acc,
    acc_q,
    load_sem,
    xload_sem,
    sib_send,
    sib_recv,
    far_send,
    far_recv,
    fwd_send,
    fwd_recv,
    pair_send,
    pair_recv,
    shr_send,
    shr_recv,
    slot_send,
    slot_recv,
    page_send,
    page_recv,
    out_sem,
):
    me = lax.axis_index("tp")
    dp = lax.axis_index("dp")
    kind = lax.rem(me, 2)
    sib = me + 1 - 2 * kind
    tok = x_hbm.shape[0]
    n_chunk = tok // CHUNK
    n_y = n_tp // 2
    tenants = wd.shape[0] // 16

    n_sub = CHUNK // SUB
    last = n_chunk - 1

    def rows(k):
        return pl.ds(pl.multiple_of(k * CHUNK, CHUNK), CHUNK)

    def unit_rows(k):
        if isinstance(k, int) and k >= last:
            return pl.ds(last * CHUNK + (k - last) * SUB, SUB)
        return rows(k)

    def remote(src, dst, ss, rs, tp_id, dp_id):
        return pltpu.make_async_remote_copy(
            src_ref=src,
            dst_ref=dst,
            send_sem=ss,
            recv_sem=rs,
            device_id={"tp": tp_id, "dp": dp_id},
            device_id_type=pl.DeviceIdType.MESH,
        )

    barrier = pltpu.get_barrier_semaphore()
    n_peers = n_tp - 1 + 2 * (n_dp - 1)
    for d in range(1, n_tp):
        pl.semaphore_signal(
            barrier,
            inc=1,
            device_id={"tp": lax.rem(me + d, n_tp), "dp": dp},
            device_id_type=pl.DeviceIdType.MESH,
        )
    for d in range(1, n_dp):
        for t in (me, sib):
            pl.semaphore_signal(
                barrier,
                inc=1,
                device_id={"tp": t, "dp": lax.rem(dp + d, n_dp)},
                device_id_type=pl.DeviceIdType.MESH,
            )

    own_load = pltpu.make_async_copy(x_hbm, xg.at[me], xload_sem)
    own_load.start()
    loads = [
        pltpu.make_async_copy(src, dst, load_sem.at[i])
        for i, (src, dst) in enumerate(
            (
                (wd_hbm, wd),
                (cache_hbm, cache),
                (wkv_hbm, wkv),
                (wup_hbm, wup),
                (wkup_hbm, wkup),
                (wq_hbm, wq),
            )
        )
    ]
    for load in loads:
        load.start()

    pl.semaphore_wait(barrier, n_peers)

    def to_sibling(k):
        return remote(
            x_hbm.at[rows(k)], xg.at[me, rows(k)], sib_send.at[k], sib_recv.at[k], sib, dp
        )

    def from_sibling(k):
        return remote(
            x_hbm.at[rows(k)], xg.at[sib, rows(k)], sib_send.at[k], sib_recv.at[k], sib, dp
        )

    def far_to(y):
        return lax.rem(me + 2 * y, n_tp)

    def far_from(y):
        return lax.rem(me + n_tp - 2 * y, n_tp)

    def to_far(k, y):
        return remote(
            x_hbm.at[unit_rows(k)],
            xg.at[me, unit_rows(k)],
            far_send.at[k, y - 1],
            far_recv.at[k, y - 1],
            far_to(y),
            dp,
        )

    def from_far(k, y):
        return remote(
            x_hbm.at[unit_rows(k)],
            xg.at[far_from(y), unit_rows(k)],
            far_send.at[k, y - 1],
            far_recv.at[k, y - 1],
            far_to(y),
            dp,
        )

    def pass_on(k, y):
        block = xg.at[far_from(y), unit_rows(k)]
        return remote(block, block, fwd_send.at[k, y - 1], fwd_recv.at[k, y - 1], sib, dp)

    def passed(k, y):
        src = lax.rem(sib + n_tp - 2 * y, n_tp)
        block = xg.at[src, unit_rows(k)]
        return remote(block, block, fwd_send.at[k, y - 1], fwd_recv.at[k, y - 1], sib, dp)

    my_y = me // 2
    span = tok // 2

    def part(c):
        return pl.ds(pl.multiple_of(c * span, span), span)

    def swap_shrink(c):
        block = pair.at[c]
        return remote(block, block, pair_send, pair_recv, sib, dp)

    def to_shrink(y, other):
        block = shp.at[my_y, :, part(kind)]
        target = lax.rem((sib if other else me) + 2 * y, n_tp)
        index = 2 * (y - 1) + other
        return remote(block, block, shr_send.at[index], shr_recv.at[index], target, dp)

    def from_shrink(y, other):
        source = lax.rem((sib if other else me) + n_tp - 2 * y, n_tp)
        half = 1 - kind if other else kind
        block = shp.at[lax.rem(my_y + n_y - y, n_y), :, part(half)]
        index = 2 * (y - 1) + other
        return remote(block, block, shr_send.at[index], shr_recv.at[index], source, dp)

    def to_slots(d):
        return remote(
            slots_own,
            slots_all.at[dp],
            slot_send.at[d - 1],
            slot_recv.at[d - 1],
            me,
            lax.rem(dp + d, n_dp),
        )

    def from_slots(d):
        src = lax.rem(dp + n_dp - d, n_dp)
        return remote(
            slots_own, slots_all.at[src], slot_send.at[d - 1], slot_recv.at[d - 1], me, src
        )

    def page_copy(k, which, other, d, replica, target_tp, target_dp):
        block = kv.at[which, replica, unit_rows(k)]
        index = other * n_dp + d
        return remote(
            block, block, page_send.at[k, index], page_recv.at[k, index], target_tp, target_dp
        )

    def page_pairs():
        return [(other, d) for other in (0, 1) for d in range(n_dp) if other or d]

    def to_pages(k, other, d):
        target = sib if other else me
        return page_copy(k, kind, other, d, dp, target, lax.rem(dp + d, n_dp))

    def from_pages(k, other, d):
        which = 1 - kind if other else kind
        src = lax.rem(dp + n_dp - d, n_dp)
        return page_copy(k, which, other, d, src, sib, src)

    for k in range(AHEAD):
        for y in range(1, n_y):
            to_far(k, y).start()

    @pl.loop(0, n_chunk)
    def _(k):
        to_sibling(k).start()

    n_pages = slots.shape[1]
    slots_own[...] = jnp.zeros(slots_own.shape, jnp.int32)
    slots_own[0:1, 0:n_pages] = slots[...]
    for d in range(1, n_dp):
        to_slots(d).start()
    slots_all[dp] = slots_own[...]

    own_load.wait()
    loads[0].wait()
    wide = 2 * CHUNK

    @pl.loop(0, tok // wide)
    def _(b):
        cols = pl.ds(pl.multiple_of(b * wide, wide), wide)
        spread = nt_dot(wd[...], xg[me, cols, :])
        group = lax.broadcasted_iota(jnp.int32, spread.shape, 0) // 16
        kept = jnp.where(group == tenant[:, cols], spread, 0.0)
        pair[kind, :, cols] = jnp.sum(kept.reshape(tenants, 16, wide), axis=0)

    swap_shrink(kind).start()

    pick = lax.broadcasted_iota(jnp.int32, (16, table_t.shape[1]), 1)
    pick = jnp.where(pick == lax.broadcasted_iota(jnp.int32, pick.shape, 0) + kind * 16, 1.0, 0.0)
    table = exact_nt(pick, table_t[...].astype(F32)).astype(jnp.int32)
    length_rows = jnp.broadcast_to(context[...].astype(F32), pick.shape)
    lengths = exact_nt(pick, length_rows)[:, 0:1].astype(jnp.int32)
    inv_scale = 1.0 / math.sqrt(128)

    def count_of(page_ids):
        lane = lax.broadcasted_iota(jnp.int32, (16, BLOCK), 1)
        offset = lane % PAGE
        total = jnp.zeros((16, BLOCK), F32)
        for p in range(16):
            hit = (table[:, p : p + 1] == page_ids) & (offset + p * PAGE < lengths)
            total += jnp.where(hit, 1.0, 0.0)
        return total

    def scores_of(keys, count):
        s = nt_dot(qs[...], keys).reshape(8, 16, count.shape[1]) * inv_scale
        return jnp.where(count[None] > 0, s, NEG)

    def weigh(s, count, m, values):
        p = count[None] * jnp.exp(s - m)
        l = jnp.sum(p, axis=2, keepdims=True)
        o = dot(p.reshape(128, count.shape[1]).astype(BF16), values)
        return l, o.reshape(8, 16, 128)

    def attend(blocks):
        scored = [scores_of(keys, count) for keys, _, count in blocks]
        m_old = m_acc[...]
        m = m_old
        for s in scored:
            m = jnp.maximum(m, jnp.max(s, axis=2, keepdims=True))
        alpha = jnp.exp(m_old - m)
        l_sum = l_acc[...] * alpha
        o_sum = o_acc[...] * alpha
        for s, (_, values, count) in zip(scored, blocks):
            l, o = weigh(s, count, m, values)
            l_sum += l
            o_sum += o
        m_acc[...] = m
        l_acc[...] = l_sum
        o_acc[...] = o_sum

    def attend_new(lo, hi):
        attend(
            [(kv[0, i, lo:hi, :], kv[1, i, lo:hi, :], counts[i, :, lo:hi]) for i in range(n_dp)]
        )

    for g in range(8):
        qs[g * 16 : (g + 1) * 16, :] = queries[:, g * 128 : (g + 1) * 128]
    m_acc[...] = jnp.full(m_acc.shape, NEG, F32)
    l_acc[...] = jnp.zeros(l_acc.shape, F32)
    o_acc[...] = jnp.zeros(o_acc.shape, F32)
    loads[1].wait()

    @pl.loop(0, pool * PAGE // BLOCK)
    def _(b):
        cols = pl.ds(pl.multiple_of(b * BLOCK, BLOCK), BLOCK)
        lane = lax.broadcasted_iota(jnp.int32, (16, BLOCK), 1)
        count = count_of((lane + b * BLOCK) // PAGE)
        attend([(cache[cols, :128], cache[cols, 128:], count)])

    swap_shrink(1 - kind).wait_recv()
    shp[my_y] = pair[0] + pair[1]
    for y in range(1, n_y):
        for other in (0, 1):
            to_shrink(y, other).start()

    for d in range(1, n_dp):
        from_slots(d).wait_recv()
    new_pages = tok // PAGE // 2
    owner_page = lax.broadcasted_iota(jnp.int32, (tok, 128), 0) // PAGE
    spread_pages = jnp.where(
        owner_page == lax.broadcasted_iota(jnp.int32, owner_page.shape, 1), 1.0, 0.0
    )

    @pl.loop(0, n_dp)
    def _(i):
        dest = exact_nt(slots_all[i].astype(F32), spread_pages).astype(jnp.int32)[0:1, :]
        mine = dest // new_pages == dp * 2 + kind
        page_ids = jnp.where(mine, dest % new_pages + pool, -1)
        counts[i] = count_of(page_ids)

    for y in range(1, n_y):
        for other in (0, 1):
            from_shrink(y, other).wait_recv()
    total = shp[0]
    for t in range(1, n_y):
        total = total + shp[t]
    shrink[...] = total.astype(BF16).astype(F32)
    for load in loads[2:]:
        load.wait()

    def near_part(k):
        cols = rows(k)
        from_sibling(k).wait_recv()
        low = jnp.broadcast_to(shrink[:, cols][None], (tenants, 16, CHUNK))
        low = low.reshape(tenants * 16, CHUNK)
        group = lax.broadcasted_iota(jnp.int32, low.shape, 0) // 16
        widened = jnp.where(group == tenant[:, cols], low, 0.0).T.astype(BF16)
        acc_kv = 0.5 * dot(widened, wkup[...])
        acc_q[...] = 0.5 * dot(widened, wup[...])
        for src in (me, sib):
            acc_kv += dot(xg[src, cols, :], wkv[src])
            acc_q[...] += dot(xg[src, cols, :], wq[src])
        return acc_kv

    def far_keys(k, cols, acc_kv):
        for y in range(1, n_y):
            src = far_from(y)
            acc_kv += dot(xg[src, cols, :], wkv[src])
        for y in range(1, n_y):
            passed(k, y).wait_recv()
            src = lax.rem(sib + n_tp - 2 * y, n_tp)
            acc_kv += dot(xg[src, cols, :], wkv[src])
        kv[kind, dp, cols, :] = acc_kv.astype(BF16)
        for other, d in page_pairs():
            to_pages(k, other, d).start()

    def far_queries(k):
        cols = rows(k)
        for y in range(1, n_y):
            for base in (me, sib):
                src = lax.rem(base + n_tp - 2 * y, n_tp)
                acc_q[...] += dot(xg[src, cols, :], wq[src])
        oq[cols, :] = acc_q[...].astype(BF16)
        pltpu.make_async_copy(oq.at[cols], out_q.at[cols], out_sem.at[k]).start()

    def arrive(k):
        for y in range(1, n_y):
            from_far(k, y).wait_recv()
            pass_on(k, y).start()

    @pl.loop(0, last)
    def _(k):
        acc_kv = near_part(k)
        arrive(k)

        @pl.when(k + AHEAD < last)
        def _():
            for y in range(1, n_y):
                to_far(k + AHEAD, y).start()

        for u in range(AHEAD):

            @pl.when(k == last - AHEAD + u)
            def _():
                for y in range(1, n_y):
                    to_far(last + u, y).start()

        far_keys(k, rows(k), acc_kv)
        far_queries(k)

    acc_last = near_part(last)

    @pl.loop(0, last)
    def _(k):
        for other, d in page_pairs():
            from_pages(k, other, d).wait_recv()

    attend_new(0, last * CHUNK)
    for u in range(n_sub):
        arrive(last + u)
        if u + AHEAD < n_sub:
            for y in range(1, n_y):
                to_far(last + u + AHEAD, y).start()
        far_keys(last + u, unit_rows(last + u), acc_last[u * SUB : (u + 1) * SUB])
    far_queries(last)
    for u in range(n_sub):
        for other, d in page_pairs():
            from_pages(last + u, other, d).wait_recv()
    attend_new(last * CHUNK, tok)
    result = (o_acc[...] / l_acc[...]).astype(BF16)
    for g in range(8):
        out_a[:, g * 128 : (g + 1) * 128] = result[g]

    for d in range(1, n_dp):
        to_slots(d).wait_send()
    swap_shrink(kind).wait_send()
    for y in range(1, n_y):
        for other in (0, 1):
            to_shrink(y, other).wait_send()

    def finish(k):
        for y in range(1, n_y):
            to_far(k, y).wait_send()
            pass_on(k, y).wait_send()
        for other, d in page_pairs():
            to_pages(k, other, d).wait_send()

    @pl.loop(0, last)
    def _(k):
        finish(k)

    for u in range(n_sub):
        finish(last + u)

    @pl.loop(0, n_chunk)
    def _(k):
        to_sibling(k).wait_send()
        pltpu.make_async_copy(oq.at[rows(k)], out_q.at[rows(k)], out_sem.at[k]).wait()


def per_device(
    n_tp,
    n_dp,
    prompt,
    query_weight,
    key_value_weight,
    adapter_down_weight,
    query_up_weight,
    adapter_up_weight,
    tenant,
    page_destination_slot,
    key_value_cache,
    queries,
    request_page_table,
    context_length,
):
    tok, feat = prompt.shape
    head = key_value_weight.shape[1]
    qcols = query_weight.shape[1]
    tenants, rank = adapter_down_weight.shape[1:]
    ranks = tenants * rank
    pool = key_value_cache.shape[2]
    half = queries.shape[2]
    n_chunk = tok // CHUNK
    down = adapter_down_weight.transpose(1, 2, 0).reshape(ranks, feat)
    hbm = pl.BlockSpec(memory_space=pl.ANY)
    vmem = pl.BlockSpec(memory_space=pltpu.VMEM)
    dma = pltpu.SemaphoreType.DMA
    n_far = n_tp // 2 - 1
    n_unit = n_chunk - 1 + CHUNK // SUB
    out_a, out_q = pl.pallas_call(
        functools.partial(kernel, n_tp, n_dp, pool),
        out_shape=(
            jax.ShapeDtypeStruct((half, queries.shape[3]), BF16),
            jax.ShapeDtypeStruct((tok, qcols), BF16),
        ),
        in_specs=[hbm] * 6 + [vmem] * 4 + [hbm, vmem],
        out_specs=(vmem, hbm),
        scratch_shapes=[
            pltpu.VMEM((n_tp, tok, feat), BF16),
            pltpu.VMEM((n_tp, feat, qcols), BF16),
            pltpu.VMEM((n_tp, feat, head), BF16),
            pltpu.VMEM((ranks, feat), BF16),
            pltpu.VMEM((ranks, qcols), BF16),
            pltpu.VMEM((ranks, head), BF16),
            pltpu.VMEM((pool * PAGE, 2 * head), BF16),
            pltpu.VMEM((tok, qcols), BF16),
            pltpu.VMEM((2, n_dp, tok, head), BF16),
            pltpu.VMEM((2, rank, tok), F32),
            pltpu.VMEM((n_tp // 2, rank, tok), F32),
            pltpu.VMEM((rank, tok), F32),
            pltpu.VMEM((n_dp, 8, 128), jnp.int32),
            pltpu.VMEM((8, 128), jnp.int32),
            pltpu.VMEM((n_dp, half, tok), F32),
            pltpu.VMEM((8 * half, head), BF16),
            pltpu.VMEM((8, half, head), F32),
            pltpu.VMEM((8, half, 1), F32),
            pltpu.VMEM((8, half, 1), F32),
            pltpu.VMEM((CHUNK, qcols), F32),
            dma((6,)),
            dma,
            dma((n_chunk,)),
            dma((n_chunk,)),
            dma((n_unit, n_far)),
            dma((n_unit, n_far)),
            dma((n_unit, n_far)),
            dma((n_unit, n_far)),
            dma,
            dma,
            dma((2 * n_far,)),
            dma((2 * n_far,)),
            dma((n_dp - 1,)),
            dma((n_dp - 1,)),
            dma((n_unit, 2 * n_dp)),
            dma((n_unit, 2 * n_dp)),
            dma((n_chunk,)),
        ],
        compiler_params=pltpu.CompilerParams(
            collective_id=0, has_side_effects=True, vmem_limit_bytes=63 * 2**20
        ),
        name="serve_layer",
    )(
        prompt,
        query_weight.reshape(n_tp, feat, qcols),
        key_value_weight.reshape(n_tp, feat, head),
        down,
        query_up_weight.reshape(ranks, qcols),
        adapter_up_weight.reshape(ranks, head),
        tenant[None, :],
        page_destination_slot[None, :],
        request_page_table.T,
        context_length[None, :],
        key_value_cache.reshape(pool * PAGE, 2 * head),
        queries.reshape(half, -1),
    )
    return out_a.reshape(1, 1, half, -1), out_q


def solution(mesh):
    in_specs = (
        P(("grp", "dp"), "tp"),
        P(None, "tp"),
        P(None, "tp"),
        P("tp", None, None),
        P(None, None, "tp"),
        P(None, None, "tp"),
        P(("grp", "dp")),
        P(("grp", "dp")),
        P(("grp", "dp"), "tp", None, None, None),
        P(("grp", "dp"), "tp", None, None),
        P(("grp", "dp"), None),
        P(("grp", "dp")),
    )
    out_specs = (P(("grp", "dp"), "tp", None, None), P(("grp", "dp"), "tp"))
    return jax.shard_map(
        functools.partial(per_device, mesh.shape["tp"], mesh.shape["dp"]),
        mesh=mesh,
        in_specs=in_specs,
        out_specs=out_specs,
        check_vma=False,
    )
```

```python
import functools
import math

import jax
import jax.numpy as jnp
from jax import lax
from jax.experimental import pallas as pl
from jax.experimental.pallas import tpu as pltpu
from jax.sharding import PartitionSpec as P

PAGE = 16
CHUNK = 128
SUB = 64
AHEAD = 4
BLOCK = 1024
NEG = -1e30
F32 = jnp.float32
BF16 = jnp.bfloat16


def nt_dot(a, b):
    return lax.dot_general(a, b, (((1,), (1,)), ((), ())), preferred_element_type=F32)


def exact_nt(a, b):
    return lax.dot_general(
        a,
        b,
        (((1,), (1,)), ((), ())),
        preferred_element_type=F32,
        precision=lax.Precision.HIGHEST,
    )


def dot(a, b):
    return jnp.dot(a, b, preferred_element_type=F32)


def kernel(
    n_tp,
    n_dp,
    pool,
    x_hbm,
    wq_hbm,
    wkv_hbm,
    wd_hbm,
    wup_hbm,
    wkup_hbm,
    tenant,
    slots,
    table_t,
    context,
    cache_hbm,
    queries,
    out_a,
    out_q,
    xg,
    wq,
    wkv,
    wd,
    wup,
    wkup,
    cache,
    oq,
    kv,
    pair,
    shp,
    shrink,
    slots_all,
    slots_own,
    counts,
    qs,
    o_acc,
    m_acc,
    l_acc,
    acc_q,
    load_sem,
    xload_sem,
    sib_send,
    sib_recv,
    far_send,
    far_recv,
    fwd_send,
    fwd_recv,
    pair_send,
    pair_recv,
    shr_send,
    shr_recv,
    slot_send,
    slot_recv,
    page_send,
    page_recv,
    out_sem,
):
    me = lax.axis_index("tp")
    dp = lax.axis_index("dp")
    kind = lax.rem(me, 2)
    sib = me + 1 - 2 * kind
    tok = x_hbm.shape[0]
    n_chunk = tok // CHUNK
    n_y = n_tp // 2
    tenants = wd.shape[0] // 16

    n_sub = CHUNK // SUB
    last = n_chunk - 1

    def rows(k):
        return pl.ds(pl.multiple_of(k * CHUNK, CHUNK), CHUNK)

    def unit_rows(k):
        if isinstance(k, int) and k >= last:
            return pl.ds(last * CHUNK + (k - last) * SUB, SUB)
        return rows(k)

    def remote(src, dst, ss, rs, tp_id, dp_id):
        return pltpu.make_async_remote_copy(
            src_ref=src,
            dst_ref=dst,
            send_sem=ss,
            recv_sem=rs,
            device_id={"tp": tp_id, "dp": dp_id},
            device_id_type=pl.DeviceIdType.MESH,
        )

    barrier = pltpu.get_barrier_semaphore()
    n_peers = n_tp - 1 + 2 * (n_dp - 1)
    for d in range(1, n_tp):
        pl.semaphore_signal(
            barrier,
            inc=1,
            device_id={"tp": lax.rem(me + d, n_tp), "dp": dp},
            device_id_type=pl.DeviceIdType.MESH,
        )
    for d in range(1, n_dp):
        for t in (me, sib):
            pl.semaphore_signal(
                barrier,
                inc=1,
                device_id={"tp": t, "dp": lax.rem(dp + d, n_dp)},
                device_id_type=pl.DeviceIdType.MESH,
            )

    own_load = pltpu.make_async_copy(x_hbm, xg.at[me], xload_sem)
    own_load.start()
    loads = [
        pltpu.make_async_copy(src, dst, load_sem.at[i])
        for i, (src, dst) in enumerate(
            (
                (wd_hbm, wd),
                (cache_hbm, cache),
                (wkv_hbm, wkv),
                (wup_hbm, wup),
                (wkup_hbm, wkup),
                (wq_hbm, wq),
            )
        )
    ]
    for load in loads:
        load.start()

    pl.semaphore_wait(barrier, n_peers)

    def to_sibling(k):
        return remote(
            x_hbm.at[rows(k)], xg.at[me, rows(k)], sib_send.at[k], sib_recv.at[k], sib, dp
        )

    def from_sibling(k):
        return remote(
            x_hbm.at[rows(k)], xg.at[sib, rows(k)], sib_send.at[k], sib_recv.at[k], sib, dp
        )

    def far_to(y):
        return lax.rem(me + 2 * y, n_tp)

    def far_from(y):
        return lax.rem(me + n_tp - 2 * y, n_tp)

    def to_far(k, y):
        return remote(
            x_hbm.at[unit_rows(k)],
            xg.at[me, unit_rows(k)],
            far_send.at[k, y - 1],
            far_recv.at[k, y - 1],
            far_to(y),
            dp,
        )

    def from_far(k, y):
        return remote(
            x_hbm.at[unit_rows(k)],
            xg.at[far_from(y), unit_rows(k)],
            far_send.at[k, y - 1],
            far_recv.at[k, y - 1],
            far_to(y),
            dp,
        )

    def pass_on(k, y):
        block = xg.at[far_from(y), unit_rows(k)]
        return remote(block, block, fwd_send.at[k, y - 1], fwd_recv.at[k, y - 1], sib, dp)

    def passed(k, y):
        src = lax.rem(sib + n_tp - 2 * y, n_tp)
        block = xg.at[src, unit_rows(k)]
        return remote(block, block, fwd_send.at[k, y - 1], fwd_recv.at[k, y - 1], sib, dp)

    my_y = me // 2
    span = tok // 2

    def part(c):
        return pl.ds(pl.multiple_of(c * span, span), span)

    def swap_shrink(c):
        block = pair.at[c]
        return remote(block, block, pair_send, pair_recv, sib, dp)

    def to_shrink(y, other):
        block = shp.at[my_y, :, part(kind)]
        target = lax.rem((sib if other else me) + 2 * y, n_tp)
        index = 2 * (y - 1) + other
        return remote(block, block, shr_send.at[index], shr_recv.at[index], target, dp)

    def from_shrink(y, other):
        source = lax.rem((sib if other else me) + n_tp - 2 * y, n_tp)
        half = 1 - kind if other else kind
        block = shp.at[lax.rem(my_y + n_y - y, n_y), :, part(half)]
        index = 2 * (y - 1) + other
        return remote(block, block, shr_send.at[index], shr_recv.at[index], source, dp)

    def to_slots(d):
        return remote(
            slots_own,
            slots_all.at[dp],
            slot_send.at[d - 1],
            slot_recv.at[d - 1],
            me,
            lax.rem(dp + d, n_dp),
        )

    def from_slots(d):
        src = lax.rem(dp + n_dp - d, n_dp)
        return remote(
            slots_own, slots_all.at[src], slot_send.at[d - 1], slot_recv.at[d - 1], me, src
        )

    def page_copy(k, which, other, d, replica, target_tp, target_dp):
        block = kv.at[which, replica, unit_rows(k)]
        index = other * n_dp + d
        return remote(
            block, block, page_send.at[k, index], page_recv.at[k, index], target_tp, target_dp
        )

    def page_pairs():
        return [(other, d) for other in (0, 1) for d in range(n_dp) if other or d]

    def to_pages(k, other, d):
        target = sib if other else me
        return page_copy(k, kind, other, d, dp, target, lax.rem(dp + d, n_dp))

    def from_pages(k, other, d):
        which = 1 - kind if other else kind
        src = lax.rem(dp + n_dp - d, n_dp)
        return page_copy(k, which, other, d, src, sib, src)

    for k in range(AHEAD):
        for y in range(1, n_y):
            to_far(k, y).start()

    @pl.loop(0, n_chunk)
    def _(k):
        to_sibling(k).start()

    n_pages = slots.shape[1]
    slots_own[...] = jnp.zeros(slots_own.shape, jnp.int32)
    slots_own[0:1, 0:n_pages] = slots[...]
    for d in range(1, n_dp):
        to_slots(d).start()
    slots_all[dp] = slots_own[...]

    own_load.wait()
    loads[0].wait()
    wide = 2 * CHUNK

    @pl.loop(0, tok // wide)
    def _(b):
        cols = pl.ds(pl.multiple_of(b * wide, wide), wide)
        spread = nt_dot(wd[...], xg[me, cols, :])
        group = lax.broadcasted_iota(jnp.int32, spread.shape, 0) // 16
        kept = jnp.where(group == tenant[:, cols], spread, 0.0)
        pair[kind, :, cols] = jnp.sum(kept.reshape(tenants, 16, wide), axis=0)

    swap_shrink(kind).start()

    pick = lax.broadcasted_iota(jnp.int32, (16, table_t.shape[1]), 1)
    pick = jnp.where(pick == lax.broadcasted_iota(jnp.int32, pick.shape, 0) + kind * 16, 1.0, 0.0)
    table = exact_nt(pick, table_t[...].astype(F32)).astype(jnp.int32)
    length_rows = jnp.broadcast_to(context[...].astype(F32), pick.shape)
    lengths = exact_nt(pick, length_rows)[:, 0:1].astype(jnp.int32)
    inv_scale = 1.0 / math.sqrt(128)

    def count_of(page_ids):
        lane = lax.broadcasted_iota(jnp.int32, (16, BLOCK), 1)
        offset = lane % PAGE
        total = jnp.zeros((16, BLOCK), F32)
        for p in range(16):
            hit = (table[:, p : p + 1] == page_ids) & (offset + p * PAGE < lengths)
            total += jnp.where(hit, 1.0, 0.0)
        return total

    def scores_of(keys, count):
        s = nt_dot(qs[...], keys).reshape(8, 16, count.shape[1]) * inv_scale
        return jnp.where(count[None] > 0, s, NEG)

    def weigh(s, count, m, values):
        p = count[None] * jnp.exp(s - m)
        l = jnp.sum(p, axis=2, keepdims=True)
        o = dot(p.reshape(128, count.shape[1]).astype(BF16), values)
        return l, o.reshape(8, 16, 128)

    def attend(blocks):
        scored = [scores_of(keys, count) for keys, _, count in blocks]
        m_old = m_acc[...]
        m = m_old
        for s in scored:
            m = jnp.maximum(m, jnp.max(s, axis=2, keepdims=True))
        alpha = jnp.exp(m_old - m)
        l_sum = l_acc[...] * alpha
        o_sum = o_acc[...] * alpha
        for s, (_, values, count) in zip(scored, blocks):
            l, o = weigh(s, count, m, values)
            l_sum += l
            o_sum += o
        m_acc[...] = m
        l_acc[...] = l_sum
        o_acc[...] = o_sum

    def attend_new(lo, hi):
        attend(
            [(kv[0, i, lo:hi, :], kv[1, i, lo:hi, :], counts[i, :, lo:hi]) for i in range(n_dp)]
        )

    for g in range(8):
        qs[g * 16 : (g + 1) * 16, :] = queries[:, g * 128 : (g + 1) * 128]
    m_acc[...] = jnp.full(m_acc.shape, NEG, F32)
    l_acc[...] = jnp.zeros(l_acc.shape, F32)
    o_acc[...] = jnp.zeros(o_acc.shape, F32)
    loads[1].wait()

    @pl.loop(0, pool * PAGE // BLOCK)
    def _(b):
        cols = pl.ds(pl.multiple_of(b * BLOCK, BLOCK), BLOCK)
        lane = lax.broadcasted_iota(jnp.int32, (16, BLOCK), 1)
        count = count_of((lane + b * BLOCK) // PAGE)
        attend([(cache[cols, :128], cache[cols, 128:], count)])

    swap_shrink(1 - kind).wait_recv()
    shp[my_y] = pair[0] + pair[1]
    for y in range(1, n_y):
        for other in (0, 1):
            to_shrink(y, other).start()

    for d in range(1, n_dp):
        from_slots(d).wait_recv()
    new_pages = tok // PAGE // 2
    owner_page = lax.broadcasted_iota(jnp.int32, (tok, 128), 0) // PAGE
    spread_pages = jnp.where(
        owner_page == lax.broadcasted_iota(jnp.int32, owner_page.shape, 1), 1.0, 0.0
    )

    @pl.loop(0, n_dp)
    def _(i):
        dest = exact_nt(slots_all[i].astype(F32), spread_pages).astype(jnp.int32)[0:1, :]
        mine = dest // new_pages == dp * 2 + kind
        page_ids = jnp.where(mine, dest % new_pages + pool, -1)
        counts[i] = count_of(page_ids)

    for y in range(1, n_y):
        for other in (0, 1):
            from_shrink(y, other).wait_recv()
    total = shp[0]
    for t in range(1, n_y):
        total = total + shp[t]
    shrink[...] = total.astype(BF16).astype(F32)
    for load in loads[2:]:
        load.wait()

    def near_part(k):
        cols = rows(k)
        from_sibling(k).wait_recv()
        low = jnp.broadcast_to(shrink[:, cols][None], (tenants, 16, CHUNK))
        low = low.reshape(tenants * 16, CHUNK)
        group = lax.broadcasted_iota(jnp.int32, low.shape, 0) // 16
        widened = jnp.where(group == tenant[:, cols], low, 0.0).T.astype(BF16)
        acc_kv = 0.5 * dot(widened, wkup[...])
        acc_q[...] = 0.5 * dot(widened, wup[...])
        for src in (me, sib):
            acc_kv += dot(xg[src, cols, :], wkv[src])
            acc_q[...] += dot(xg[src, cols, :], wq[src])
        return acc_kv

    def far_keys(k, cols, acc_kv):
        for y in range(1, n_y):
            src = far_from(y)
            acc_kv += dot(xg[src, cols, :], wkv[src])
        for y in range(1, n_y):
            passed(k, y).wait_recv()
            src = lax.rem(sib + n_tp - 2 * y, n_tp)
            acc_kv += dot(xg[src, cols, :], wkv[src])
        kv[kind, dp, cols, :] = acc_kv.astype(BF16)
        for other, d in page_pairs():
            to_pages(k, other, d).start()

    def far_queries(k):
        cols = rows(k)
        for y in range(1, n_y):
            for base in (me, sib):
                src = lax.rem(base + n_tp - 2 * y, n_tp)
                acc_q[...] += dot(xg[src, cols, :], wq[src])
        oq[cols, :] = acc_q[...].astype(BF16)
        pltpu.make_async_copy(oq.at[cols], out_q.at[cols], out_sem.at[k]).start()

    def arrive(k):
        for y in range(1, n_y):
            from_far(k, y).wait_recv()
            pass_on(k, y).start()

    @pl.loop(0, last)
    def _(k):
        acc_kv = near_part(k)
        arrive(k)

        @pl.when(k + AHEAD < last)
        def _():
            for y in range(1, n_y):
                to_far(k + AHEAD, y).start()

        for u in range(min(AHEAD, n_sub)):

            @pl.when(k == last - AHEAD + u)
            def _():
                for y in range(1, n_y):
                    to_far(last + u, y).start()

        far_keys(k, rows(k), acc_kv)
        far_queries(k)

    acc_last = near_part(last)

    @pl.loop(0, last)
    def _(k):
        for other, d in page_pairs():
            from_pages(k, other, d).wait_recv()

    attend_new(0, last * CHUNK)
    for u in range(n_sub):
        arrive(last + u)
        if u + AHEAD < n_sub:
            for y in range(1, n_y):
                to_far(last + u + AHEAD, y).start()
        far_keys(last + u, unit_rows(last + u), acc_last[u * SUB : (u + 1) * SUB])
    far_queries(last)
    for u in range(n_sub):
        for other, d in page_pairs():
            from_pages(last + u, other, d).wait_recv()
    attend_new(last * CHUNK, tok)
    result = (o_acc[...] / l_acc[...]).astype(BF16)
    for g in range(8):
        out_a[:, g * 128 : (g + 1) * 128] = result[g]

    for d in range(1, n_dp):
        to_slots(d).wait_send()
    swap_shrink(kind).wait_send()
    for y in range(1, n_y):
        for other in (0, 1):
            to_shrink(y, other).wait_send()

    def finish(k):
        for y in range(1, n_y):
            to_far(k, y).wait_send()
            pass_on(k, y).wait_send()
        for other, d in page_pairs():
            to_pages(k, other, d).wait_send()

    @pl.loop(0, last)
    def _(k):
        finish(k)

    for u in range(n_sub):
        finish(last + u)

    @pl.loop(0, n_chunk)
    def _(k):
        to_sibling(k).wait_send()
        pltpu.make_async_copy(oq.at[rows(k)], out_q.at[rows(k)], out_sem.at[k]).wait()


def per_device(
    n_tp,
    n_dp,
    prompt,
    query_weight,
    key_value_weight,
    adapter_down_weight,
    query_up_weight,
    adapter_up_weight,
    tenant,
    page_destination_slot,
    key_value_cache,
    queries,
    request_page_table,
    context_length,
):
    tok, feat = prompt.shape
    head = key_value_weight.shape[1]
    qcols = query_weight.shape[1]
    tenants, rank = adapter_down_weight.shape[1:]
    ranks = tenants * rank
    pool = key_value_cache.shape[2]
    half = queries.shape[2]
    n_chunk = tok // CHUNK
    down = adapter_down_weight.transpose(1, 2, 0).reshape(ranks, feat)
    hbm = pl.BlockSpec(memory_space=pl.ANY)
    vmem = pl.BlockSpec(memory_space=pltpu.VMEM)
    dma = pltpu.SemaphoreType.DMA
    n_far = n_tp // 2 - 1
    n_unit = n_chunk - 1 + CHUNK // SUB
    out_a, out_q = pl.pallas_call(
        functools.partial(kernel, n_tp, n_dp, pool),
        out_shape=(
            jax.ShapeDtypeStruct((half, queries.shape[3]), BF16),
            jax.ShapeDtypeStruct((tok, qcols), BF16),
        ),
        in_specs=[hbm] * 6 + [vmem] * 4 + [hbm, vmem],
        out_specs=(vmem, hbm),
        scratch_shapes=[
            pltpu.VMEM((n_tp, tok, feat), BF16),
            pltpu.VMEM((n_tp, feat, qcols), BF16),
            pltpu.VMEM((n_tp, feat, head), BF16),
            pltpu.VMEM((ranks, feat), BF16),
            pltpu.VMEM((ranks, qcols), BF16),
            pltpu.VMEM((ranks, head), BF16),
            pltpu.VMEM((pool * PAGE, 2 * head), BF16),
            pltpu.VMEM((tok, qcols), BF16),
            pltpu.VMEM((2, n_dp, tok, head), BF16),
            pltpu.VMEM((2, rank, tok), F32),
            pltpu.VMEM((n_tp // 2, rank, tok), F32),
            pltpu.VMEM((rank, tok), F32),
            pltpu.VMEM((n_dp, 8, 128), jnp.int32),
            pltpu.VMEM((8, 128), jnp.int32),
            pltpu.VMEM((n_dp, half, tok), F32),
            pltpu.VMEM((8 * half, head), BF16),
            pltpu.VMEM((8, half, head), F32),
            pltpu.VMEM((8, half, 1), F32),
            pltpu.VMEM((8, half, 1), F32),
            pltpu.VMEM((CHUNK, qcols), F32),
            dma((6,)),
            dma,
            dma((n_chunk,)),
            dma((n_chunk,)),
            dma((n_unit, n_far)),
            dma((n_unit, n_far)),
            dma((n_unit, n_far)),
            dma((n_unit, n_far)),
            dma,
            dma,
            dma((2 * n_far,)),
            dma((2 * n_far,)),
            dma((n_dp - 1,)),
            dma((n_dp - 1,)),
            dma((n_unit, 2 * n_dp)),
            dma((n_unit, 2 * n_dp)),
            dma((n_chunk,)),
        ],
        compiler_params=pltpu.CompilerParams(
            collective_id=0, has_side_effects=True, vmem_limit_bytes=63 * 2**20
        ),
        name="serve_layer",
    )(
        prompt,
        query_weight.reshape(n_tp, feat, qcols),
        key_value_weight.reshape(n_tp, feat, head),
        down,
        query_up_weight.reshape(ranks, qcols),
        adapter_up_weight.reshape(ranks, head),
        tenant[None, :],
        page_destination_slot[None, :],
        request_page_table.T,
        context_length[None, :],
        key_value_cache.reshape(pool * PAGE, 2 * head),
        queries.reshape(half, -1),
    )
    return out_a.reshape(1, 1, half, -1), out_q


def solution(mesh):
    in_specs = (
        P(("grp", "dp"), "tp"),
        P(None, "tp"),
        P(None, "tp"),
        P("tp", None, None),
        P(None, None, "tp"),
        P(None, None, "tp"),
        P(("grp", "dp")),
        P(("grp", "dp")),
        P(("grp", "dp"), "tp", None, None, None),
        P(("grp", "dp"), "tp", None, None),
        P(("grp", "dp"), None),
        P(("grp", "dp")),
    )
    out_specs = (P(("grp", "dp"), "tp", None, None), P(("grp", "dp"), "tp"))
    return jax.shard_map(
        functools.partial(per_device, mesh.shape["tp"], mesh.shape["dp"]),
        mesh=mesh,
        in_specs=in_specs,
        out_specs=out_specs,
        check_vma=False,
    )
```
